512 devices in a mesh: ct: 128 (over y, z, core), bl: 4 (over x).
Axes of the slice: x: 4, y: 8, z: 8, core: 2. Of those that a mesh axis runs over, the one named last changes fastest.
Arguments:
- samples: bfloat16 [1024, 65536], P('ct', 'bl'), may hold values from -6 to 6
- history: bfloat16 [1024, 1536], P('ct'), may hold values from -6 to 6
- tile_cell: int32 [256, 36], P('ct'), may hold values from 0 to 7
- tile_weight: float32 [256, 36], P('ct'), may hold values from 0.25 to 4
Outputs:
- grid: float32 [8, 256, 2, 128, 128], P('bl', 'ct')
The draws below stay inside these ranges and needn't reach their ends.
All inputs are finite; a program needn't handle non-finite values.
Results may differ from the reference program's by a relative error of at most 0.0048.
Values may be sent and summed in bfloat16 or wider, within the bound.
A program may use at most 64 MiB of HBM per device.

```python
import math
import jax
import jax.numpy as jnp
import numpy as np
from jax import lax

CH = 256
BLOCK = 128
TAPS = 4
SPECTRA = 128
FRAME = 512
INPUTS = 1024
NTILE = 36
NCELL = 8


def touch_ends(values, own_key, low, largest):
    spot = [jax.random.randint(jax.random.fold_in(own_key, axis), (), 0, length) for axis, length in enumerate(values.shape)]
    main_axis = values.shape.index(max(values.shape))
    next_to = spot[:main_axis] + [(spot[main_axis] + 1) % values.shape[main_axis]] + spot[main_axis + 1:]
    return values.at[tuple(spot)].set(low).at[tuple(next_to)].set(largest)


def shard_levels(key, shape, cuts, least, high):
    loudness, own = 1.0, jax.random.fold_in(key, 6)
    for dim, parts in cuts:
        heights = jnp.exp(jax.random.uniform(jax.random.fold_in(own, dim), (parts,), jnp.float32, least / len(cuts), high / len(cuts)))
        loudness = loudness * jnp.repeat(heights, shape[dim] // parts).reshape([-1 if axis == dim else 1 for axis in range(len(shape))])
    return loudness


def rank_bounds(amount, slope):
    weights = [(1 << 20) // math.isqrt(grade ** slope) + 1 for grade in range(1, amount + 1)]
    scale = 1 + sum(weights) // (1 << 30)
    return np.cumsum(np.array([max(1, weight // scale) for weight in weights]))


def ranked_ids(stream_key, shape, count, skew):
    listing = rank_bounds(count, skew)
    lot = jax.random.randint(jax.random.fold_in(stream_key, 1), shape, 0, int(listing[count - 1]))
    standing = jnp.searchsorted(jnp.asarray(listing, jnp.int32), lot, side="right")
    return jax.random.permutation(jax.random.fold_in(stream_key, 2), count)[standing].astype(jnp.int32)


def scatter_about(stream_key, shape, scale, limit, pieces=(), kind=jnp.bfloat16):
    result = scale * jax.random.normal(stream_key, shape, jnp.float32)
    if pieces:
        result = result * shard_levels(stream_key, shape, pieces, -0.22, 0.18)
    return jnp.clip(result, -limit, limit).astype(kind)


def setup_inputs(seed: int = 0) -> dict:
    streams_of = jax.random.split(jax.random.key(seed), 5)
    samples = scatter_about(streams_of[0], (INPUTS, SPECTRA * FRAME), 1.0, 6.0, ((0, 128), (1, 4)))
    history = scatter_about(streams_of[1], (INPUTS, (TAPS - 1) * FRAME), 1.0, 6.0, ((0, 128),))
    tile_cell = touch_ends(ranked_ids(streams_of[2], (CH, NTILE), NCELL, 2), jax.random.fold_in(streams_of[2], 3), 0, NCELL - 1).astype(jnp.int32)
    tile_weight = jnp.clip(jnp.exp(math.log(4.0) - 2.7725887 * jax.random.uniform(streams_of[3], (CH, NTILE), jnp.float32) ** shard_levels(streams_of[3], (CH, NTILE), ((0, 128),), -0.2, 0.2)), 0.25, 4.0)
    return dict(samples=samples, history=history, tile_cell=tile_cell, tile_weight=tile_weight)


def filter_table():
    span = TAPS * FRAME
    sample_pos = jnp.arange(span, dtype=jnp.float32) + 0.5
    window = jnp.sinc(sample_pos / FRAME - TAPS / 2.0) * (0.5 - 0.5 * jnp.cos(2.0 * math.pi * sample_pos / span))
    phase_int = jnp.arange(FRAME, dtype=jnp.int32)[:, None] * jnp.arange(CH, dtype=jnp.int32)[None, :] % FRAME
    angle = phase_int.astype(jnp.float32) * (2.0 * math.pi / FRAME)
    basis = jnp.concatenate([jnp.cos(angle), -jnp.sin(angle)], axis=1)
    table = window.reshape(TAPS, FRAME)[:, :, None] * basis[None] * (2.0 / math.sqrt(FRAME))
    return table.astype(jnp.bfloat16)

def reference(samples, history, tile_cell, tile_weight):
    blocks = INPUTS // BLOCK
    table = filter_table().astype(jnp.float32)
    whole = jnp.concatenate([history, samples], axis=1).reshape(blocks, BLOCK, SPECTRA + TAPS - 1, FRAME)

    def one_block(group):
        group_wide = group.astype(jnp.float32)
        accum = jnp.zeros((2 * CH, BLOCK, SPECTRA), jnp.float32)
        for tap_index in range(TAPS):
            accum = accum + jnp.einsum('psn,nk->kps', group_wide[:, tap_index:tap_index + SPECTRA], table[tap_index], precision=lax.Precision.HIGHEST)
        return accum.astype(jnp.bfloat16)
    spectra = lax.map(one_block, whole)
    spectra = spectra.reshape(blocks, 2, CH, BLOCK, SPECTRA).transpose(2, 1, 0, 3, 4).reshape(CH, 2, INPUTS, SPECTRA)
    row_list = []
    col_list = []
    for row_block in range(blocks):
        for col_block in range(row_block, blocks):
            row_list.append(row_block)
            col_list.append(col_block)
    rows_np = np.array(row_list, dtype=np.int32)
    cols_np = np.array(col_list, dtype=np.int32)
    cell_ids = jnp.arange(NCELL, dtype=jnp.int32)
    norm_scale = 1.0 / math.sqrt(SPECTRA)

    def one_channel(items):
        chan, cells_row, weight_row = items
        data = chan.astype(jnp.float32)
        products = jnp.einsum('aps,bqs->abpq', data, data, precision=lax.Precision.HIGHEST)
        real_part = products[0, 0] + products[1, 1]
        imag_part = products[1, 0] - products[0, 1]
        visibility = jnp.stack([real_part, imag_part]).reshape(2, blocks, BLOCK, blocks, BLOCK)
        tiles = visibility[:, rows_np, :, cols_np, :]
        selector = (cells_row[None, :] == cell_ids[:, None]).astype(jnp.float32) * (weight_row * norm_scale)[None, :]
        return jnp.einsum('et,txpq->expq', selector, tiles, precision=lax.Precision.HIGHEST)
    grid = lax.map(one_channel, (spectra, tile_cell, tile_weight))
    return grid.transpose(1, 0, 2, 3, 4)
```

```python
import functools
import math

import jax
import jax.numpy as jnp
import numpy as np
from jax import lax
from jax.experimental import pallas as pl
from jax.experimental.pallas import tpu as pltpu
from jax.sharding import PartitionSpec as P

MESH = pl.DeviceIdType.MESH
BF16 = jnp.bfloat16
F32 = jnp.float32

CH = 256
BLOCK = 128
TAPS = 4
SPECTRA = 128
FRAME = 512
NTILE = 36
CELL_DEV = 2
RING = 8
NX = 4
ROWS = 8
SPEC_DEV = SPECTRA // NX
HALO = TAPS - 1
OFFSETS = (4, 3, 5, 2, 6, 1, 7)


def filter_table():
    span = TAPS * FRAME
    pos = np.arange(span, dtype=np.float32) + np.float32(0.5)
    window = np.sinc(pos / np.float32(FRAME) - np.float32(TAPS / 2.0)).astype(np.float32) * (
        np.float32(0.5) - np.float32(0.5) * np.cos(np.float32(2.0 * math.pi) * pos / np.float32(span))
    )
    phase = np.arange(FRAME)[:, None] * np.arange(CH)[None, :] % FRAME
    angle = phase.astype(np.float32) * np.float32(2.0 * math.pi / FRAME)
    basis = np.concatenate([np.cos(angle), -np.sin(angle)], axis=1).astype(np.float32)
    table = window.astype(np.float32).reshape(TAPS, FRAME)[:, :, None] * basis[None]
    table = table * np.float32(2.0 / math.sqrt(FRAME))
    part, core, chip = np.meshgrid(np.arange(4), np.arange(2), np.arange(64), indexing="ij")
    column = (part % 2) * CH + 2 * (2 * chip + core) + part // 2
    return np.ascontiguousarray(table[:, :, column.reshape(-1)].transpose(0, 2, 1)).astype(BF16)


def swap_step(pair, bit, lane):
    low, high = pair
    clear = (lane & bit) == 0
    return (
        jnp.where(clear, low, pltpu.roll(high, bit, 1)),
        jnp.where(clear, pltpu.roll(low, 128 - bit, 1), high),
    )


def kernel(
    samples, history, table, cells, weights, out,
    tab, smp, halo, even, odd, spec, turn, hold, mid, full, rhs, lhs, wsm,
    tab_sem, smp_sem, halo_send, halo_recv, core_sem, own_sem, p1_send, p1_recv, p2_send, p2_recv, ag_send, ag_recv,
):
    ct = lax.axis_index("ct")
    bl = lax.axis_index("bl")
    y = ct // 16
    z = lax.rem(ct // 2, RING)
    c = lax.rem(ct, 2)

    def on(yy, zz, cc):
        return (yy * 16 + zz * 2 + cc, bl)

    barrier = pltpu.get_barrier_semaphore()

    def greet(device):
        pl.semaphore_signal(barrier, inc=1, device_id=device, device_id_type=MESH)

    for k in range(1, NX):
        greet((ct, lax.rem(bl + k, NX)))
    greet(on(y, z, 1 - c))
    for k in range(1, RING):
        greet(on(lax.rem(y + k, RING), z, c))
        greet(on(y, lax.rem(z + k, RING), c))

    smp_copy = pltpu.make_async_copy(samples, smp, smp_sem)
    smp_copy.start()
    tab_copies = []
    for t in range(TAPS):
        tab_copies.append(pltpu.make_async_copy(table.at[t], tab.at[t], tab_sem.at[t]))
        tab_copies[-1].start()

    def one_weight(t, carry):
        for ch in range(2):
            scaled = weights[ch, t] * (1.0 / math.sqrt(SPECTRA))
            for e in range(CELL_DEV):
                wsm[ch, e, t] = jnp.where(cells[ch, t] == bl * CELL_DEV + e, scaled, 0.0)
        return carry

    lax.fori_loop(0, NTILE, one_weight, 0)

    pl.semaphore_wait(barrier, NX - 1 + 1 + 2 * (RING - 1))

    halo_copy = pltpu.make_async_remote_copy(
        src_ref=samples.at[:, pl.ds((SPEC_DEV - HALO) * FRAME, HALO * FRAME)],
        dst_ref=halo,
        send_sem=halo_send,
        recv_sem=halo_recv,
        device_id=(ct, lax.rem(bl + 1, NX)),
        device_id_type=MESH,
    )
    hist_copy = pltpu.make_async_copy(history, halo, own_sem.at[2])

    @pl.when(bl < NX - 1)
    def _():
        halo_copy.start()

    @pl.when(bl == 0)
    def _():
        hist_copy.start()

    def put(ext, value):
        even[pl.ds(8 * ext, 8), :] = value
        if ext >= 1:
            odd[pl.ds(8 * (ext - 1), 8), :] = value

    smp_copy.wait()
    for f in range(SPEC_DEV):
        put(f + HALO, smp[:, pl.ds(f * FRAME, FRAME)])

    @pl.when(bl < NX - 1)
    def _():
        halo_copy.wait_send()

    @pl.when(bl == 0)
    def _():
        hist_copy.wait()

    @pl.when(bl > 0)
    def _():
        halo_copy.wait_recv()

    for f in range(HALO):
        put(f, halo[:, pl.ds(f * FRAME, FRAME)])

    total = None
    for t in range(TAPS):
        tab_copies[t].wait()
        source = (even, odd)[t % 2]
        term = lax.dot_general(
            tab[t], source[pl.ds(16 * (t // 2), 256), :], (((1,), (1,)), ((), ())), preferred_element_type=F32
        )
        total = term if total is None else total + term
    spec[...] = total

    lane = lax.broadcasted_iota(jnp.int32, (8, 128), 1)
    for g in range(16):
        v = [spec[pl.ds(q * 128 + g * 8, 8), pl.ds(h * 128, 128)] for q in range(4) for h in range(2)]
        for bit in (1, 2, 4):
            for i in range(8):
                if not i & bit:
                    v[i], v[i | bit] = swap_step((v[i], v[i | bit]), bit, lane)
        for p in range(ROWS):
            turn[pl.ds(g * 64 + p, 8, stride=8), :] = v[p]
        core = g // 8
        other = lax.rem(c + core, 2)
        slot = core * (1 - other) + 2 * other
        chips = g % 8
        hold[slot, chips] = turn[pl.ds(g * 64, 64), :].astype(BF16).reshape(8, 8, 128)

    swap = pltpu.make_async_remote_copy(
        src_ref=hold.at[2], dst_ref=hold.at[c], send_sem=core_sem.at[0], recv_sem=core_sem.at[1],
        device_id=on(y, z, 1 - c), device_id_type=MESH,
    )
    swap.start()
    swap.wait_recv()

    def turn_corner(first_is_z):
        me1, me2 = (z, y) if first_is_z else (y, z)

        def there(phase, k):
            if (phase == 1) == first_is_z:
                return on(y, lax.rem(z + k, RING), c)
            return on(lax.rem(y + k, RING), z, c)

        def part(ref, i, by_z):
            return ref.at[:, :, i] if by_z else ref.at[:, i]

        both = hold.at[pl.ds(0, 2)]
        mine = full.at[bl]
        first = []
        for n, k in enumerate(OFFSETS):
            first.append(pltpu.make_async_remote_copy(
                src_ref=part(both, lax.rem(me1 + k, RING), first_is_z), dst_ref=part(mid, me1, first_is_z),
                send_sem=p1_send.at[n], recv_sem=p1_recv.at[n], device_id=there(1, k), device_id_type=MESH,
            ))
            first[-1].start()
        keep = pltpu.make_async_copy(part(both, me1, first_is_z), part(mid, me1, first_is_z), own_sem.at[0])
        keep.start()
        for copy in first:
            copy.wait_recv()
        keep.wait()
        second = []
        for n, k in enumerate(OFFSETS):
            second.append(pltpu.make_async_remote_copy(
                src_ref=part(mid, lax.rem(me2 + k, RING), not first_is_z), dst_ref=part(mine, me2, not first_is_z),
                send_sem=p2_send.at[n], recv_sem=p2_recv.at[n], device_id=there(2, k), device_id_type=MESH,
            ))
            second[-1].start()
        keep = pltpu.make_async_copy(part(mid, me2, not first_is_z), part(mine, me2, not first_is_z), own_sem.at[1])
        keep.start()
        spread = []
        for n, k in enumerate((0,) + OFFSETS):
            if n == 0:
                keep.wait()
            else:
                second[n - 1].wait_recv()
            chunk = part(mine, lax.rem(me2 + RING - k, RING), not first_is_z)
            for o in (2, 1, 3):
                spread.append(pltpu.make_async_remote_copy(
                    src_ref=chunk, dst_ref=chunk, send_sem=ag_send.at[o - 1, n], recv_sem=ag_recv.at[o - 1, n],
                    device_id=(ct, lax.rem(bl + o, NX)), device_id_type=MESH,
                ))
                spread[-1].start()
        for copy in spread:
            copy.wait_recv()
        for copy in first + second + spread:
            copy.wait_send()

    @pl.when(c == 0)
    def _():
        turn_corner(True)

    @pl.when(c == 1)
    def _():
        turn_corner(False)

    swap.wait_send()

    lane = lax.broadcasted_iota(jnp.int32, (16, 128), 1)
    real = (lane & 2) == 0

    def operands(n, carry):
        j, zz = n // RING, lax.rem(n, RING)
        rows = pl.ds(pl.multiple_of(zz * 16, 16), 16)
        under = pl.ds(pl.multiple_of(128 + zz * 16, 16), 16)
        d = [full[b, :, j, zz].astype(F32).reshape(16, 128) for b in range(NX)]
        for half in range(2):
            pair = swap_step((d[2 * half], d[2 * half + 1]), 4, lane)
            for ch in range(2):
                x = pair[ch]
                r = jnp.where(real, -pltpu.roll(x, 126, 1), pltpu.roll(x, 2, 1))
                cols = pl.ds(pl.multiple_of(j * 256 + half * 128, 128), 128)
                rhs[ch, rows, cols] = x.astype(BF16)
                rhs[ch, under, cols] = r.astype(BF16)
        return carry

    lax.fori_loop(0, RING * RING, operands, 0)

    def fold(zz, carry):
        rows = pl.ds(pl.multiple_of(zz * 16, 16), 16)
        for ch in range(2):
            x = [rhs[ch, rows, i * 256:(i + 1) * 256].astype(F32) for i in range(8)]
            for e in range(CELL_DEV):
                place = pl.ds(pl.multiple_of(e * 128 + zz * 16, 16), 16)
                for j in range(8):
                    acc = None
                    for i in range(j + 1):
                        t = i * 8 - i * (i - 1) // 2 + j - i
                        term = x[i] * wsm[ch, e, t]
                        acc = term if acc is None else acc + term
                    lhs[ch, place, j * 256:(j + 1) * 256] = acc.astype(BF16)
        return carry

    lax.fori_loop(0, RING, fold, 0)

    for ch in range(2):
        result = lax.dot_general(lhs[ch], rhs[ch], (((1,), (1,)), ((), ())), preferred_element_type=F32)
        for e in range(CELL_DEV):
            for x in range(2):
                out[e, ch, x] = result[e * 128:(e + 1) * 128, x * 128:(x + 1) * 128]


def shards(samples, history, tile_cell, tile_weight):
    table = jnp.asarray(filter_table())
    any_space = pl.BlockSpec(memory_space=pl.ANY)
    smem = pl.BlockSpec(memory_space=pltpu.SMEM)
    dma = pltpu.SemaphoreType.DMA
    return pl.pallas_call(
        kernel,
        out_shape=jax.ShapeDtypeStruct((CELL_DEV, 2, 2, BLOCK, BLOCK), F32),
        in_specs=[any_space, any_space, any_space, smem, smem],
        out_specs=pl.BlockSpec(memory_space=pltpu.VMEM),
        scratch_shapes=[
            pltpu.VMEM((TAPS, 2 * CH, FRAME), BF16),
            pltpu.VMEM((8, SPEC_DEV * FRAME), BF16),
            pltpu.VMEM((8, HALO * FRAME), BF16),
            pltpu.VMEM((288, FRAME), BF16),
            pltpu.VMEM((288, FRAME), BF16),
            pltpu.VMEM((512, 256), F32),
            pltpu.VMEM((1024, 128), F32),
            pltpu.VMEM((3, RING, RING, 8, 128), BF16),
            pltpu.VMEM((2, RING, RING, 8, 128), BF16),
            pltpu.VMEM((NX, 2, RING, RING, 8, 128), BF16),
            pltpu.VMEM((2, 256, 2048), BF16),
            pltpu.VMEM((2, 256, 2048), BF16),
            pltpu.SMEM((2, CELL_DEV, NTILE), F32),
            dma((TAPS,)),
            dma,
            dma,
            dma,
            dma((2,)),
            dma((3,)),
            dma((RING - 1,)),
            dma((RING - 1,)),
            dma((RING - 1,)),
            dma((RING - 1,)),
            dma((NX - 1, RING)),
            dma((NX - 1, RING)),
        ],
        compiler_params=pltpu.CompilerParams(
            collective_id=0, has_side_effects=True, vmem_limit_bytes=60 * 1024 * 1024
        ),
    )(samples, history, table, tile_cell, tile_weight)


def solution(mesh):
    return jax.shard_map(
        shards,
        mesh=mesh,
        in_specs=(P("ct", "bl"), P("ct", None), P("ct", None), P("ct", None)),
        out_specs=P("bl", "ct", None, None, None),
        check_vma=False,
    )
```

```python
import functools
import math

import jax
import jax.numpy as jnp
import numpy as np
from jax import lax
from jax.experimental import pallas as pl
from jax.experimental.pallas import tpu as pltpu
from jax.sharding import PartitionSpec as P

MESH = pl.DeviceIdType.MESH
BF16 = jnp.bfloat16
F32 = jnp.float32

CH = 256
BLOCK = 128
TAPS = 4
SPECTRA = 128
FRAME = 512
NTILE = 36
CELL_DEV = 2
RING = 8
NX = 4
ROWS = 8
SPEC_DEV = SPECTRA // NX
HALO = TAPS - 1
UNROLL = 8
OFFSETS = (4, 3, 5, 2, 6, 1, 7)


def filter_table():
    span = TAPS * FRAME
    pos = np.arange(span, dtype=np.float32) + np.float32(0.5)
    window = np.sinc(pos / np.float32(FRAME) - np.float32(TAPS / 2.0)).astype(np.float32) * (
        np.float32(0.5) - np.float32(0.5) * np.cos(np.float32(2.0 * math.pi) * pos / np.float32(span))
    )
    phase = np.arange(FRAME)[:, None] * np.arange(CH)[None, :] % FRAME
    angle = phase.astype(np.float32) * np.float32(2.0 * math.pi / FRAME)
    basis = np.concatenate([np.cos(angle), -np.sin(angle)], axis=1).astype(np.float32)
    table = window.astype(np.float32).reshape(TAPS, FRAME)[:, :, None] * basis[None]
    table = table * np.float32(2.0 / math.sqrt(FRAME))
    part, core, chip = np.meshgrid(np.arange(4), np.arange(2), np.arange(64), indexing="ij")
    column = (part % 2) * CH + 2 * (2 * chip + core) + part // 2
    return np.ascontiguousarray(table[:, :, column.reshape(-1)].transpose(0, 2, 1)).astype(BF16)


def swap_step(pair, bit, lane):
    low, high = pair
    clear = (lane & bit) == 0
    return (
        jnp.where(clear, low, pltpu.roll(high, bit, 1)),
        jnp.where(clear, pltpu.roll(low, 128 - bit, 1), high),
    )


def kernel(
    samples, history, table, cells_hbm, weights_hbm, out,
    tab, smp, halo, even, odd, spec, turn, hold, mid, full, rhs, lhs, wsm, cells, weights,
    tab_sem, smp_sem, cell_sem, halo_send, halo_recv, core_sem, own_sem, p1_send, p1_recv, p2_send, p2_recv, ag_send, ag_recv,
):
    ct = lax.axis_index("ct")
    bl = lax.axis_index("bl")
    y = ct // 16
    z = lax.rem(ct // 2, RING)
    c = lax.rem(ct, 2)

    def on(yy, zz, cc):
        return (yy * 16 + zz * 2 + cc, bl)

    barrier = pltpu.get_barrier_semaphore()

    def greet(device):
        pl.semaphore_signal(barrier, inc=1, device_id=device, device_id_type=MESH)

    for k in range(1, NX):
        greet((ct, lax.rem(bl + k, NX)))
    greet(on(y, z, 1 - c))
    for k in range(1, RING):
        greet(on(lax.rem(y + k, RING), z, c))
        greet(on(y, lax.rem(z + k, RING), c))

    smp_copy = pltpu.make_async_copy(samples, smp, smp_sem)
    smp_copy.start()
    cell_copies = [
        pltpu.make_async_copy(cells_hbm, cells, cell_sem.at[0]),
        pltpu.make_async_copy(weights_hbm, weights, cell_sem.at[1]),
    ]
    for copy in cell_copies:
        copy.start()
    tab_copies = []
    for t in range(TAPS):
        tab_copies.append(pltpu.make_async_copy(table.at[t], tab.at[t], tab_sem.at[t]))
        tab_copies[-1].start()

    pl.semaphore_wait(barrier, NX - 1 + 1 + 2 * (RING - 1))

    halo_copy = pltpu.make_async_remote_copy(
        src_ref=samples.at[:, pl.ds((SPEC_DEV - HALO) * FRAME, HALO * FRAME)],
        dst_ref=halo,
        send_sem=halo_send,
        recv_sem=halo_recv,
        device_id=(ct, lax.rem(bl + 1, NX)),
        device_id_type=MESH,
    )
    hist_copy = pltpu.make_async_copy(history, halo, own_sem.at[4])

    @pl.when(bl < NX - 1)
    def _():
        halo_copy.start()

    @pl.when(bl == 0)
    def _():
        hist_copy.start()

    def put(ext, value):
        even[pl.ds(8 * ext, 8), :] = value
        if ext >= 1:
            odd[pl.ds(8 * (ext - 1), 8), :] = value

    smp_copy.wait()
    for f in range(SPEC_DEV):
        put(f + HALO, smp[:, pl.ds(f * FRAME, FRAME)])

    @pl.when(bl < NX - 1)
    def _():
        halo_copy.wait_send()

    @pl.when(bl == 0)
    def _():
        hist_copy.wait()

    @pl.when(bl > 0)
    def _():
        halo_copy.wait_recv()

    for f in range(HALO):
        put(f, halo[:, pl.ds(f * FRAME, FRAME)])

    total = None
    for t in range(TAPS):
        tab_copies[t].wait()
        source = (even, odd)[t % 2]
        term = lax.dot_general(
            tab[t], source[pl.ds(16 * (t // 2), 256), :], (((1,), (1,)), ((), ())), preferred_element_type=F32
        )
        total = term if total is None else total + term
    spec[...] = total

    lane = lax.broadcasted_iota(jnp.int32, (8, 128), 1)
    for g in range(16):
        v = [spec[pl.ds(q * 128 + g * 8, 8), pl.ds(h * 128, 128)] for q in range(4) for h in range(2)]
        for bit in (1, 2, 4):
            for i in range(8):
                if not i & bit:
                    v[i], v[i | bit] = swap_step((v[i], v[i | bit]), bit, lane)
        for p in range(ROWS):
            turn[pl.ds(g * 64 + p, 8, stride=8), :] = v[p]
        core = g // 8
        other = lax.rem(c + core, 2)
        slot = core * (1 - other) + 2 * other
        chips = g % 8
        hold[slot, chips] = turn[pl.ds(g * 64, 64), :].astype(BF16).reshape(8, 8, 128)

    swap = pltpu.make_async_remote_copy(
        src_ref=hold.at[2], dst_ref=hold.at[c], send_sem=core_sem.at[0], recv_sem=core_sem.at[1],
        device_id=on(y, z, 1 - c), device_id_type=MESH,
    )
    swap.start()

    for copy in cell_copies:
        copy.wait()

    def one_weight(t, carry):
        for ch in range(2):
            scaled = weights[ch, t] * (1.0 / math.sqrt(SPECTRA))
            for e in range(CELL_DEV):
                wsm[ch, e, t] = jnp.where(cells[ch, t] == bl * CELL_DEV + e, scaled, 0.0)
        return carry

    lax.fori_loop(0, NTILE, one_weight, 0)

    lane16 = lax.broadcasted_iota(jnp.int32, (16, 128), 1)
    real = (lane16 & 2) == 0

    def operands(j, zz):
        rows = pl.ds(pl.multiple_of(zz * 16, 16), 16)
        under = pl.ds(pl.multiple_of(128 + zz * 16, 16), 16)
        d = [full[b, :, j, zz].astype(F32).reshape(16, 128) for b in range(NX)]
        for half in range(2):
            pair = swap_step((d[2 * half], d[2 * half + 1]), 4, lane16)
            for ch in range(2):
                x = pair[ch]
                r = jnp.where(real, -pltpu.roll(x, 126, 1), pltpu.roll(x, 2, 1))
                cols = pl.ds(pl.multiple_of(j * 256 + half * 128, 128), 128)
                rhs[ch, rows, cols] = x.astype(BF16)
                rhs[ch, under, cols] = r.astype(BF16)

    def turn_corner(mine_core):
        first_is_z = mine_core == 0
        me1, me2 = (z, y) if first_is_z else (y, z)

        def there(phase, k):
            if (phase == 1) == first_is_z:
                return on(y, lax.rem(z + k, RING), c)
            return on(lax.rem(y + k, RING), z, c)

        def part(ref, i, phase):
            return ref.at[:, i] if (phase == 1) == first_is_z else ref.at[i]

        first, keep1, second, keep2, spread = [], [], [], [], {}

        def start_first(h):
            source, target = hold.at[(mine_core + h) % 2], mid.at[(mine_core + h) % 2]
            copies = [
                pltpu.make_async_remote_copy(
                    src_ref=part(source, lax.rem(me1 + k, RING), 1), dst_ref=part(target, me1, 1),
                    send_sem=p1_send.at[h, n], recv_sem=p1_recv.at[h, n], device_id=there(1, k), device_id_type=MESH,
                )
                for n, k in enumerate(OFFSETS)
            ]
            for copy in copies:
                copy.start()
            keep = pltpu.make_async_copy(part(source, me1, 1), part(target, me1, 1), own_sem.at[h])
            keep.start()
            first.append(copies)
            keep1.append(keep)

        def share(h, n, k, source):
            target = part(full.at[bl, (mine_core + h) % 2], lax.rem(me2 + RING - k, RING), 2)
            copies = [
                pltpu.make_async_remote_copy(
                    src_ref=target if source is None else source, dst_ref=target,
                    send_sem=ag_send.at[o - 1, h, n], recv_sem=ag_recv.at[o - 1, h, n],
                    device_id=(ct, lax.rem(bl + o, NX)), device_id_type=MESH,
                )
                for o in (2, 1, 3)
            ]
            for copy in copies:
                copy.start()
            spread[h, n] = copies

        def start_second(h):
            source, target = mid.at[(mine_core + h) % 2], full.at[bl, (mine_core + h) % 2]
            for copy in first[h]:
                copy.wait_recv()
            keep1[h].wait()
            copies = [
                pltpu.make_async_remote_copy(
                    src_ref=part(source, lax.rem(me2 + k, RING), 2), dst_ref=part(target, me2, 2),
                    send_sem=p2_send.at[h, n], recv_sem=p2_recv.at[h, n], device_id=there(2, k), device_id_type=MESH,
                )
                for n, k in enumerate(OFFSETS)
            ]
            for copy in copies:
                copy.start()
            share(h, 0, 0, part(source, me2, 2))
            keep = pltpu.make_async_copy(part(source, me2, 2), part(target, me2, 2), own_sem.at[2 + h])
            keep.start()
            second.append(copies)
            keep2.append(keep)

        start_first(0)
        swap.wait_recv()
        start_first(1)
        start_second(0)
        start_second(1)
        for h in range(2):
            for n, k in enumerate(OFFSETS):
                second[h][n].wait_recv()
                share(h, n + 1, k, None)
        keep2[0].wait()
        keep2[1].wait()
        for n, k in enumerate((0,) + OFFSETS):
            for h in range(2):
                for copy in spread[h, n]:
                    copy.wait_recv()
            chunk = lax.rem(me2 + RING - k, RING)

            def one(i, carry):
                if first_is_z:
                    operands(chunk, i)
                else:
                    operands(i, chunk)
                return carry

            lax.fori_loop(0, RING, one, 0, unroll=UNROLL)
        for h in range(2):
            for copy in first[h] + second[h]:
                copy.wait_send()
            for n in range(RING):
                for copy in spread[h, n]:
                    copy.wait_send()

    @pl.when(c == 0)
    def _():
        turn_corner(0)

    @pl.when(c == 1)
    def _():
        turn_corner(1)

    swap.wait_send()

    def fold(zz, carry):
        rows = pl.ds(pl.multiple_of(zz * 16, 16), 16)
        for ch in range(2):
            x = [rhs[ch, rows, i * 256:(i + 1) * 256].astype(F32) for i in range(8)]
            for e in range(CELL_DEV):
                place = pl.ds(pl.multiple_of(e * 128 + zz * 16, 16), 16)
                for j in range(8):
                    acc = None
                    for i in range(j + 1):
                        t = i * 8 - i * (i - 1) // 2 + j - i
                        term = x[i] * wsm[ch, e, t]
                        acc = term if acc is None else acc + term
                    lhs[ch, place, j * 256:(j + 1) * 256] = acc.astype(BF16)
        return carry

    lax.fori_loop(0, RING, fold, 0)

    for ch in range(2):
        result = lax.dot_general(lhs[ch], rhs[ch], (((1,), (1,)), ((), ())), preferred_element_type=F32)
        for e in range(CELL_DEV):
            for x in range(2):
                out[e, ch, x] = result[e * 128:(e + 1) * 128, x * 128:(x + 1) * 128]


def shards(samples, history, tile_cell, tile_weight):
    table = jnp.asarray(filter_table())
    hbm = pl.BlockSpec(memory_space=pltpu.HBM)
    dma = pltpu.SemaphoreType.DMA
    return pl.pallas_call(
        kernel,
        out_shape=jax.ShapeDtypeStruct((CELL_DEV, 2, 2, BLOCK, BLOCK), F32),
        in_specs=[hbm] * 5,
        out_specs=pl.BlockSpec(memory_space=pltpu.VMEM),
        scratch_shapes=[
            pltpu.VMEM((TAPS, 2 * CH, FRAME), BF16),
            pltpu.VMEM((8, SPEC_DEV * FRAME), BF16),
            pltpu.VMEM((8, HALO * FRAME), BF16),
            pltpu.VMEM((288, FRAME), BF16),
            pltpu.VMEM((288, FRAME), BF16),
            pltpu.VMEM((512, 256), F32),
            pltpu.VMEM((1024, 128), F32),
            pltpu.VMEM((3, RING, RING, 8, 128), BF16),
            pltpu.VMEM((2, RING, RING, 8, 128), BF16),
            pltpu.VMEM((NX, 2, RING, RING, 8, 128), BF16),
            pltpu.VMEM((2, 256, 2048), BF16),
            pltpu.VMEM((2, 256, 2048), BF16),
            pltpu.SMEM((2, CELL_DEV, NTILE), F32),
            pltpu.SMEM((2, NTILE), jnp.int32),
            pltpu.SMEM((2, NTILE), F32),
            dma((TAPS,)),
            dma,
            dma((2,)),
            dma,
            dma,
            dma((2,)),
            dma((5,)),
            dma((2, RING - 1)),
            dma((2, RING - 1)),
            dma((2, RING - 1)),
            dma((2, RING - 1)),
            dma((NX - 1, 2, RING)),
            dma((NX - 1, 2, RING)),
        ],
        compiler_params=pltpu.CompilerParams(
            collective_id=0, has_side_effects=True, vmem_limit_bytes=40 * 1024 * 1024
        ),
    )(*[pltpu.with_memory_space_constraint(v, pltpu.HBM) for v in (samples, history, table, tile_cell, tile_weight)])


def solution(mesh):
    return jax.shard_map(
        shards,
        mesh=mesh,
        in_specs=(P("ct", "bl"), P("ct", None), P("ct", None), P("ct", None)),
        out_specs=P("bl", "ct", None, None, None),
        check_vma=False,
    )
```

```python
import functools
import math

import jax
import jax.numpy as jnp
import numpy as np
from jax import lax
from jax.experimental import pallas as pl
from jax.experimental.pallas import tpu as pltpu
from jax.sharding import PartitionSpec as P

MESH = pl.DeviceIdType.MESH
BF16 = jnp.bfloat16
F32 = jnp.float32

CH = 256
BLOCK = 128
TAPS = 4
SPECTRA = 128
FRAME = 512
NTILE = 36
CELL_DEV = 2
RING = 8
NX = 4
ROWS = 8
SPEC_DEV = SPECTRA // NX
HALO = TAPS - 1


def offset(n):
    m = n - 1
    odd = m % 2
    return (1 - (n == 0)) * (4 + (1 - odd) * (m // 2) - odd * ((m + 1) // 2))


OFFSETS = tuple(offset(n) for n in range(1, RING))


def filter_table():
    span = TAPS * FRAME
    pos = np.arange(span, dtype=np.float32) + np.float32(0.5)
    window = np.sinc(pos / np.float32(FRAME) - np.float32(TAPS / 2.0)).astype(np.float32) * (
        np.float32(0.5) - np.float32(0.5) * np.cos(np.float32(2.0 * math.pi) * pos / np.float32(span))
    )
    phase = np.arange(FRAME)[:, None] * np.arange(CH)[None, :] % FRAME
    angle = phase.astype(np.float32) * np.float32(2.0 * math.pi / FRAME)
    basis = np.concatenate([np.cos(angle), -np.sin(angle)], axis=1).astype(np.float32)
    table = window.astype(np.float32).reshape(TAPS, FRAME)[:, :, None] * basis[None]
    table = table * np.float32(2.0 / math.sqrt(FRAME))
    part, core, chip = np.meshgrid(np.arange(4), np.arange(2), np.arange(64), indexing="ij")
    column = (part % 2) * CH + 2 * (2 * chip + core) + part // 2
    return np.ascontiguousarray(table[:, :, column.reshape(-1)].transpose(0, 2, 1)).astype(BF16)


def swap_step(pair, bit, lane):
    low, high = pair
    clear = (lane & bit) == 0
    return (
        jnp.where(clear, low, pltpu.roll(high, bit, 1)),
        jnp.where(clear, pltpu.roll(low, 128 - bit, 1), high),
    )


def kernel(
    samples, history, table, cells_hbm, weights_hbm, out,
    tab, smp, halo, even, odd, spec, turn, hold, mid, relay, full, perm, rhs, lhs, wsm, cells, weights,
    tab_sem, smp_sem, cell_sem, halo_send, halo_recv, own_sem, p1_send, p1_recv, p2_send, p2_recv, a_send, a_recv,
    b_send, b_recv,
):
    ct = lax.axis_index("ct")
    bl = lax.axis_index("bl")
    y = ct // 16
    z = lax.rem(ct // 2, RING)
    c = lax.rem(ct, 2)

    def on(yy, zz, cc):
        return (yy * 16 + zz * 2 + cc, bl)

    barrier = pltpu.get_barrier_semaphore()

    def greet(device):
        pl.semaphore_signal(barrier, inc=1, device_id=device, device_id_type=MESH)

    for k in (1, NX - 1):
        greet((ct, lax.rem(bl + k, NX)))
        greet(on(y, z, 1 - c)[:1] + (lax.rem(bl + k, NX),))
    greet(on(y, z, 1 - c))
    for k in range(1, RING):
        greet(on(lax.rem(y + k, RING), z, c))
        greet(on(y, lax.rem(z + k, RING), c))

    smp_copy = pltpu.make_async_copy(samples, smp, smp_sem)
    smp_copy.start()
    cell_copies = [
        pltpu.make_async_copy(cells_hbm, cells, cell_sem.at[0]),
        pltpu.make_async_copy(weights_hbm, weights, cell_sem.at[1]),
    ]
    for copy in cell_copies:
        copy.start()
    tab_copies = []
    for t in range(TAPS):
        tab_copies.append(pltpu.make_async_copy(table.at[t], tab.at[t], tab_sem.at[t]))
        tab_copies[-1].start()

    pl.semaphore_wait(barrier, 5 + 2 * (RING - 1))

    halo_copy = pltpu.make_async_remote_copy(
        src_ref=samples.at[:, pl.ds((SPEC_DEV - HALO) * FRAME, HALO * FRAME)],
        dst_ref=halo,
        send_sem=halo_send,
        recv_sem=halo_recv,
        device_id=(ct, lax.rem(bl + 1, NX)),
        device_id_type=MESH,
    )
    hist_copy = pltpu.make_async_copy(history, halo, own_sem.at[4])

    @pl.when(bl < NX - 1)
    def _():
        halo_copy.start()

    @pl.when(bl == 0)
    def _():
        hist_copy.start()

    def put(ext, value):
        even[pl.ds(8 * ext, 8), :] = value
        if ext >= 1:
            odd[pl.ds(8 * (ext - 1), 8), :] = value

    smp_copy.wait()
    for f in range(SPEC_DEV):
        put(f + HALO, smp[:, pl.ds(f * FRAME, FRAME)])

    @pl.when(bl < NX - 1)
    def _():
        halo_copy.wait_send()

    @pl.when(bl == 0)
    def _():
        hist_copy.wait()

    @pl.when(bl > 0)
    def _():
        halo_copy.wait_recv()

    for f in range(HALO):
        put(f, halo[:, pl.ds(f * FRAME, FRAME)])

    total = None
    for t in range(TAPS):
        tab_copies[t].wait()
        source = (even, odd)[t % 2]
        term = lax.dot_general(
            tab[t], source[pl.ds(16 * (t // 2), 256), :], (((1,), (1,)), ((), ())), preferred_element_type=F32
        )
        total = term if total is None else total + term
    spec[...] = total

    lane = lax.broadcasted_iota(jnp.int32, (8, 128), 1)
    for g in range(16):
        v = [spec[pl.ds(q * 128 + g * 8, 8), pl.ds(h * 128, 128)] for q in range(4) for h in range(2)]
        for bit in (1, 2, 4):
            for i in range(8):
                if not i & bit:
                    v[i], v[i | bit] = swap_step((v[i], v[i | bit]), bit, lane)
        for p in range(ROWS):
            turn[pl.ds(g * 64 + p, 8, stride=8), :] = v[p]
        hold[g // 8, g % 8] = turn[pl.ds(g * 64, 64), :].astype(BF16).reshape(8, 8, 128)

    def column(k):
        return lax.rem(y + RING - k, RING)

    def depth(k):
        return lax.rem(z + RING - k, RING)

    first = {}
    for n, k in enumerate(OFFSETS):
        far_y, far_z = lax.rem(y + k, RING), lax.rem(z + k, RING)
        first[0, n] = pltpu.make_async_remote_copy(
            src_ref=hold.at[c, :, far_z], dst_ref=mid.at[0, :, z],
            send_sem=p1_send.at[0, n], recv_sem=p1_recv.at[0, n], device_id=on(y, far_z, c), device_id_type=MESH,
        )
        first[1, n] = pltpu.make_async_remote_copy(
            src_ref=hold.at[1 - c, far_y], dst_ref=mid.at[1, y],
            send_sem=p1_send.at[1, n], recv_sem=p1_recv.at[1, n], device_id=on(far_y, z, c), device_id_type=MESH,
        )
        first[0, n].start()
        first[1, n].start()
    keep = [
        pltpu.make_async_copy(hold.at[c, :, z], mid.at[0, :, z], own_sem.at[0]),
        pltpu.make_async_copy(hold.at[1 - c, y], mid.at[1, y], own_sem.at[1]),
        pltpu.make_async_copy(mid.at[0, y], full.at[bl, c, y], own_sem.at[2]),
    ]
    keep[0].start()
    keep[1].start()

    for copy in cell_copies:
        copy.wait()

    def one_weight(t, carry):
        for ch in range(2):
            scaled = weights[ch, t] * (1.0 / math.sqrt(SPECTRA))
            for e in range(CELL_DEV):
                wsm[ch, e, t] = jnp.where(cells[ch, t] == bl * CELL_DEV + e, scaled, 0.0)
        return carry

    lax.fori_loop(0, NTILE, one_weight, 0)

    source = lax.broadcasted_iota(jnp.int32, (256, 512), 0)
    column_id = lax.broadcasted_iota(jnp.int32, (256, 512), 1)
    turned, channel = column_id // 256, (column_id // 128) % 2
    lane_id = (column_id % 128) ^ (2 * turned)
    wanted = ((lane_id // 4) % 2) * 128 + (lane_id & 123) + 4 * channel
    sign = 1 - 2 * turned * (lane_id // 2 % 2)
    perm[...] = jnp.where(source == wanted, sign, 0).astype(F32).astype(BF16)

    right, left = lax.rem(bl + 1, NX), lax.rem(bl + NX - 1, NX)
    sent = list(first.values())

    def push(source, target, send, recv, device):
        copy = pltpu.make_async_remote_copy(
            src_ref=source, dst_ref=target, send_sem=send, recv_sem=recv, device_id=device, device_id_type=MESH
        )
        copy.start()
        sent.append(copy)
        return copy

    def wait_for(sem):
        pltpu.make_async_remote_copy(
            src_ref=relay.at[0], dst_ref=relay.at[0], send_sem=own_sem.at[3], recv_sem=sem,
            device_id=(ct, right), device_id_type=MESH,
        ).wait_recv()

    def share_own(n, k, source):
        target = full.at[bl, c, column(k)]
        source = target if source is None else source
        push(source, target, a_send.at[0, n], a_recv.at[0, n], (ct, right))
        push(source, target, a_send.at[1, n], a_recv.at[1, n], (ct, left))

    def share_other(n, k, source):
        target = full.at[bl, c, :, depth(k)]
        source = relay.at[:, depth(k)] if source is None else source
        push(source, target, b_send.at[0, n], b_recv.at[0, n], on(y, z, 1 - c)[:1] + (right,))
        push(source, target, b_send.at[1, n], b_recv.at[1, n], on(y, z, 1 - c)[:1] + (left,))
        push(source, target, b_send.at[2, n], b_recv.at[2, n], on(y, z, 1 - c))

    def pass_own(n, k):
        wait_for(a_recv.at[0, n])
        chunk = full.at[left, c, column(k)]
        push(chunk, chunk, a_send.at[2, n], a_recv.at[2, n], (ct, right))

    def pass_other(n):
        chunk = full.at[right, 1 - c, :, depth(offset(n))]
        return pltpu.make_async_remote_copy(
            src_ref=chunk, dst_ref=chunk, send_sem=b_send.at[3, n], recv_sem=b_recv.at[3, n],
            device_id=(ct, left), device_id_type=MESH,
        )

    second = {}
    for h in range(2):
        for n in range(RING - 1):
            first[h, n].wait_recv()
        keep[h].wait()
        for n, k in enumerate(OFFSETS):
            far_y, far_z = lax.rem(y + k, RING), lax.rem(z + k, RING)
            if h == 0:
                second[h, n] = push(
                    mid.at[0, far_y], full.at[bl, c, y], p2_send.at[0, n], p2_recv.at[0, n], on(far_y, z, c)
                )
            else:
                second[h, n] = push(
                    mid.at[1, :, far_z], relay.at[:, z], p2_send.at[1, n], p2_recv.at[1, n], on(y, far_z, c)
                )
        if h == 0:
            share_own(0, 0, mid.at[0, y])
            keep[2].start()
        else:
            share_other(0, 0, mid.at[1, :, z])
    for n, k in enumerate(OFFSETS):
        second[0, n].wait_recv()
        share_own(n + 1, k, None)
    for n, k in enumerate(OFFSETS):
        second[1, n].wait_recv()
        share_other(n + 1, k, None)
    for n, k in enumerate((0,) + OFFSETS):
        pass_own(n, k)
    for n in range(RING):
        wait_for(b_recv.at[1, n])
        pass_other(n).start()
    keep[2].wait()
    for n in range(RING):
        wait_for(a_recv.at[1, n])
        wait_for(b_recv.at[0, n])
        wait_for(b_recv.at[2, n])

    def operands(pair, time, j):
        d = [
            jnp.concatenate([full[2 * time + b, :, jj, zz].reshape(16, 128) for jj in (j, j + 1) for zz in range(RING)], axis=0)
            for b in range(2)
        ]
        moved = jnp.dot(jnp.concatenate(d, axis=1), perm[...], preferred_element_type=F32).astype(BF16)
        for jj in range(2):
            for ch in range(2):
                for part in range(2):
                    rhs[pair, ch, part * 128:(part + 1) * 128, (j + jj) * 128:(j + jj + 1) * 128] = moved[
                        jj * 128:(jj + 1) * 128, part * 256 + ch * 128:part * 256 + (ch + 1) * 128
                    ]

    def fold(pair, zz):
        rows = pl.ds(pl.multiple_of(zz * 16, 16), 16)
        for ch in range(2):
            x = [rhs[pair, ch, rows, i * 128:(i + 1) * 128].astype(F32) for i in range(8)]
            for e in range(CELL_DEV):
                place = pl.ds(pl.multiple_of(e * 128 + zz * 16, 16), 16)
                for j in range(8):
                    acc = None
                    for i in range(j + 1):
                        t = i * 8 - i * (i - 1) // 2 + j - i
                        term = x[i] * wsm[ch, e, t]
                        acc = term if acc is None else acc + term
                    lhs[pair, ch, place, j * 128:(j + 1) * 128] = acc.astype(BF16)

    def products(pair, time):
        def slab(zz, carry):
            fold(pair, zz)
            return carry

        for j in range(0, 8, 2):
            operands(pair, time, j)
        lax.fori_loop(0, RING, slab, 0)
        for ch in range(2):
            result = lax.dot_general(
                lhs[pair, ch], rhs[pair, ch], (((1,), (1,)), ((), ())), preferred_element_type=F32
            )
            for e in range(CELL_DEV):
                for x in range(2):
                    value = result[e * 128:(e + 1) * 128, x * 128:(x + 1) * 128]
                    out[e, ch, x] = value if pair == 0 else out[e, ch, x] + value

    products(0, bl // 2)
    for n in range(RING):
        wait_for(a_recv.at[2, n])
        wait_for(b_recv.at[3, n])
    products(1, 1 - bl // 2)

    for copy in sent:
        copy.wait_send()
    for n in range(RING):
        pass_other(n).wait_send()


def shards(samples, history, tile_cell, tile_weight):
    table = jnp.asarray(filter_table())
    hbm = pl.BlockSpec(memory_space=pltpu.HBM)
    dma = pltpu.SemaphoreType.DMA
    return pl.pallas_call(
        kernel,
        out_shape=jax.ShapeDtypeStruct((CELL_DEV, 2, 2, BLOCK, BLOCK), F32),
        in_specs=[hbm] * 5,
        out_specs=pl.BlockSpec(memory_space=pltpu.VMEM),
        scratch_shapes=[
            pltpu.VMEM((TAPS, 2 * CH, FRAME), BF16),
            pltpu.VMEM((8, SPEC_DEV * FRAME), BF16),
            pltpu.VMEM((8, HALO * FRAME), BF16),
            pltpu.VMEM((288, FRAME), BF16),
            pltpu.VMEM((288, FRAME), BF16),
            pltpu.VMEM((512, 256), F32),
            pltpu.VMEM((1024, 128), F32),
            pltpu.VMEM((2, RING, RING, 8, 128), BF16),
            pltpu.VMEM((2, RING, RING, 8, 128), BF16),
            pltpu.VMEM((RING, RING, 8, 128), BF16),
            pltpu.VMEM((NX, 2, RING, RING, 8, 128), BF16),
            pltpu.VMEM((256, 512), BF16),
            pltpu.VMEM((2, 2, 256, 1024), BF16),
            pltpu.VMEM((2, 2, 256, 1024), BF16),
            pltpu.SMEM((2, CELL_DEV, NTILE), F32),
            pltpu.SMEM((2, NTILE), jnp.int32),
            pltpu.SMEM((2, NTILE), F32),
            dma((TAPS,)),
            dma,
            dma((2,)),
            dma,
            dma,
            dma((5,)),
            dma((2, RING - 1)),
            dma((2, RING - 1)),
            dma((2, RING - 1)),
            dma((2, RING - 1)),
            dma((3, RING)),
            dma((3, RING)),
            dma((4, RING)),
            dma((4, RING)),
        ],
        compiler_params=pltpu.CompilerParams(
            collective_id=0, has_side_effects=True, vmem_limit_bytes=40 * 1024 * 1024
        ),
    )(*[pltpu.with_memory_space_constraint(v, pltpu.HBM) for v in (samples, history, table, tile_cell, tile_weight)])


def solution(mesh):
    return jax.shard_map(
        shards,
        mesh=mesh,
        in_specs=(P("ct", "bl"), P("ct", None), P("ct", None), P("ct", None)),
        out_specs=P("bl", "ct", None, None, None),
        check_vma=False,
    )
```

```python
import functools
import math

import jax
import jax.numpy as jnp
import numpy as np
from jax import lax
from jax.experimental import pallas as pl
from jax.experimental.pallas import tpu as pltpu
from jax.sharding import PartitionSpec as P

MESH = pl.DeviceIdType.MESH
BF16 = jnp.bfloat16
F32 = jnp.float32

CH = 256
BLOCK = 128
TAPS = 4
SPECTRA = 128
FRAME = 512
NTILE = 36
CELL_DEV = 2
RING = 8
NX = 4
ROWS = 8
SPEC_DEV = SPECTRA // NX
HALO = TAPS - 1


def offset(n):
    m = n - 1
    odd = m % 2
    return (1 - (n == 0)) * (4 + (1 - odd) * (m // 2) - odd * ((m + 1) // 2))


OFFSETS = tuple(offset(n) for n in range(1, RING))
NEAREST = tuple(reversed(tuple(enumerate(OFFSETS))))


def filter_table():
    span = TAPS * FRAME
    pos = np.arange(span, dtype=np.float32) + np.float32(0.5)
    window = np.sinc(pos / np.float32(FRAME) - np.float32(TAPS / 2.0)).astype(np.float32) * (
        np.float32(0.5) - np.float32(0.5) * np.cos(np.float32(2.0 * math.pi) * pos / np.float32(span))
    )
    phase = np.arange(FRAME)[:, None] * np.arange(CH)[None, :] % FRAME
    angle = phase.astype(np.float32) * np.float32(2.0 * math.pi / FRAME)
    basis = np.concatenate([np.cos(angle), -np.sin(angle)], axis=1).astype(np.float32)
    table = window.astype(np.float32).reshape(TAPS, FRAME)[:, :, None] * basis[None]
    table = table * np.float32(2.0 / math.sqrt(FRAME))
    part, core, chip = np.meshgrid(np.arange(4), np.arange(2), np.arange(64), indexing="ij")
    column = (part % 2) * CH + 2 * (2 * chip + core) + part // 2
    rows = table[:, :, column.reshape(-1)].transpose(2, 0, 1).reshape(2 * CH, span)
    return np.ascontiguousarray(rows).astype(BF16)


def swap_step(pair, bit, lane):
    low, high = pair
    clear = (lane & bit) == 0
    return (
        jnp.where(clear, low, pltpu.roll(high, bit, 1)),
        jnp.where(clear, pltpu.roll(low, 128 - bit, 1), high),
    )


def kernel(
    samples, history, table, cells_hbm, weights_hbm, out,
    tab, smp, halo, taps, spec, turn, hold, mid, relay, full, perm, rhs, lhs, wsm, cells, weights,
    tab_sem, smp_sem, cell_sem, halo_send, halo_recv, own_sem, p1_send, p1_recv, p2_send, p2_recv, a_send, a_recv,
    b_send, b_recv,
):
    ct = lax.axis_index("ct")
    bl = lax.axis_index("bl")
    y = ct // 16
    z = lax.rem(ct // 2, RING)
    c = lax.rem(ct, 2)

    def on(yy, zz, cc):
        return (yy * 16 + zz * 2 + cc, bl)

    barrier = pltpu.get_barrier_semaphore()

    def greet(device):
        pl.semaphore_signal(barrier, inc=1, device_id=device, device_id_type=MESH)

    for k in (1, NX - 1):
        greet((ct, lax.rem(bl + k, NX)))
        greet(on(y, z, 1 - c)[:1] + (lax.rem(bl + k, NX),))
    greet(on(y, z, 1 - c))
    for k in range(1, RING):
        greet(on(lax.rem(y + k, RING), z, c))
        greet(on(y, lax.rem(z + k, RING), c))

    smp_copy = pltpu.make_async_copy(samples, smp, smp_sem)
    smp_copy.start()
    cell_copies = [
        pltpu.make_async_copy(cells_hbm, cells, cell_sem.at[0]),
        pltpu.make_async_copy(weights_hbm, weights, cell_sem.at[1]),
    ]
    for copy in cell_copies:
        copy.start()
    tab_copy = pltpu.make_async_copy(table, tab, tab_sem)
    tab_copy.start()

    pl.semaphore_wait(barrier, 5 + 2 * (RING - 1))

    halo_copy = pltpu.make_async_remote_copy(
        src_ref=samples.at[:, pl.ds((SPEC_DEV - HALO) * FRAME, HALO * FRAME)],
        dst_ref=halo,
        send_sem=halo_send,
        recv_sem=halo_recv,
        device_id=(ct, lax.rem(bl + 1, NX)),
        device_id_type=MESH,
    )
    hist_copy = pltpu.make_async_copy(history, halo, own_sem.at[4])

    @pl.when(bl < NX - 1)
    def _():
        halo_copy.start()

    @pl.when(bl == 0)
    def _():
        hist_copy.start()

    def put(ext, value):
        for t in range(TAPS):
            if 0 <= ext - t < SPEC_DEV:
                taps[pl.ds(8 * (ext - t), 8), t * FRAME:(t + 1) * FRAME] = value

    smp_copy.wait()
    for f in range(SPEC_DEV):
        put(f + HALO, smp[:, pl.ds(f * FRAME, FRAME)])

    @pl.when(bl < NX - 1)
    def _():
        halo_copy.wait_send()

    @pl.when(bl == 0)
    def _():
        hist_copy.wait()

    @pl.when(bl > 0)
    def _():
        halo_copy.wait_recv()

    for f in range(HALO):
        put(f, halo[:, pl.ds(f * FRAME, FRAME)])

    tab_copy.wait()
    spec[...] = lax.dot_general(tab[...], taps[...], (((1,), (1,)), ((), ())), preferred_element_type=F32)

    lane = lax.broadcasted_iota(jnp.int32, (8, 128), 1)
    def column(k):
        return lax.rem(y + RING - k, RING)

    def depth(k):
        return lax.rem(z + RING - k, RING)

    def to_rows(core, which, chips):
        at = core * 64 + chips * 8
        v = [
            spec[pl.ds(pl.multiple_of(q * 128 + at, 8), 8), pl.ds(h * 128, 128)]
            for q in range(4)
            for h in range(2)
        ]
        for bit in (1, 2, 4):
            for i in range(8):
                if not i & bit:
                    v[i], v[i | bit] = swap_step((v[i], v[i | bit]), bit, lane)
        place = which * 512 + chips * 64
        for p in range(ROWS):
            turn[pl.ds(place + p, 8, stride=8), :] = v[p]
        hold[which, chips] = turn[pl.ds(place, 64), :].astype(BF16).reshape(8, 8, 128)

    first = {}
    for chips in range(8):
        to_rows(c, 0, chips)
    for n, k in enumerate(OFFSETS):
        far_z = lax.rem(z + k, RING)
        first[0, n] = pltpu.make_async_remote_copy(
            src_ref=hold.at[0, :, far_z], dst_ref=mid.at[0, :, z],
            send_sem=p1_send.at[0, n], recv_sem=p1_recv.at[0, n], device_id=on(y, far_z, c), device_id_type=MESH,
        )
        first[0, n].start()
    for chips in range(8):
        to_rows(1 - c, 1, chips)
    for n, k in enumerate(OFFSETS):
        far_y = lax.rem(y + k, RING)
        first[1, n] = pltpu.make_async_remote_copy(
            src_ref=hold.at[1, far_y], dst_ref=mid.at[1, y],
            send_sem=p1_send.at[1, n], recv_sem=p1_recv.at[1, n], device_id=on(far_y, z, c), device_id_type=MESH,
        )
        first[1, n].start()
    keep = [
        pltpu.make_async_copy(hold.at[0, :, z], mid.at[0, :, z], own_sem.at[0]),
        pltpu.make_async_copy(hold.at[1, y], mid.at[1, y], own_sem.at[1]),
        pltpu.make_async_copy(mid.at[0, y], full.at[bl, c, y], own_sem.at[2]),
    ]
    keep[0].start()
    keep[1].start()

    for copy in cell_copies:
        copy.wait()

    def one_weight(t, carry):
        for ch in range(2):
            scaled = weights[ch, t] * (1.0 / math.sqrt(SPECTRA))
            for e in range(CELL_DEV):
                wsm[ch, e, t] = jnp.where(cells[ch, t] == bl * CELL_DEV + e, scaled, 0.0)
        return carry

    lax.fori_loop(0, NTILE, one_weight, 0)

    source = lax.broadcasted_iota(jnp.int32, (256, 512), 0)
    column_id = lax.broadcasted_iota(jnp.int32, (256, 512), 1)
    turned, channel = column_id // 256, (column_id // 128) % 2
    lane_id = (column_id % 128) ^ (2 * turned)
    wanted = ((lane_id // 4) % 2) * 128 + (lane_id & 123) + 4 * channel
    sign = 1 - 2 * turned * (lane_id // 2 % 2)
    perm[...] = jnp.where(source == wanted, sign, 0).astype(F32).astype(BF16)

    right, left = lax.rem(bl + 1, NX), lax.rem(bl + NX - 1, NX)
    sent = list(first.values())

    def push(source, target, send, recv, device):
        copy = pltpu.make_async_remote_copy(
            src_ref=source, dst_ref=target, send_sem=send, recv_sem=recv, device_id=device, device_id_type=MESH
        )
        copy.start()
        sent.append(copy)
        return copy

    def wait_for(sem):
        pltpu.make_async_remote_copy(
            src_ref=relay.at[0], dst_ref=relay.at[0], send_sem=own_sem.at[3], recv_sem=sem,
            device_id=(ct, right), device_id_type=MESH,
        ).wait_recv()

    def share_own(n, k, source):
        target = full.at[bl, c, column(k)]
        source = target if source is None else source
        push(source, target, a_send.at[0, n], a_recv.at[0, n], (ct, right))
        push(source, target, a_send.at[1, n], a_recv.at[1, n], (ct, left))

    def share_other(n, k, source):
        target = full.at[bl, c, :, depth(k)]
        source = relay.at[:, depth(k)] if source is None else source
        push(source, target, b_send.at[0, n], b_recv.at[0, n], on(y, z, 1 - c)[:1] + (right,))
        push(source, target, b_send.at[1, n], b_recv.at[1, n], on(y, z, 1 - c)[:1] + (left,))
        push(source, target, b_send.at[2, n], b_recv.at[2, n], on(y, z, 1 - c))

    def pass_own(n, k):
        wait_for(a_recv.at[0, n])
        chunk = full.at[left, c, column(k)]
        push(chunk, chunk, a_send.at[2, n], a_recv.at[2, n], (ct, right))

    def pass_other(n):
        chunk = full.at[right, 1 - c, :, depth(offset(n))]
        return pltpu.make_async_remote_copy(
            src_ref=chunk, dst_ref=chunk, send_sem=b_send.at[3, n], recv_sem=b_recv.at[3, n],
            device_id=(ct, left), device_id_type=MESH,
        )

    second = {}
    for h in range(2):
        for n in range(RING - 1):
            first[h, n].wait_recv()
        keep[h].wait()
        for n, k in enumerate(OFFSETS):
            far_y, far_z = lax.rem(y + k, RING), lax.rem(z + k, RING)
            if h == 0:
                second[h, n] = push(
                    mid.at[0, far_y], full.at[bl, c, y], p2_send.at[0, n], p2_recv.at[0, n], on(far_y, z, c)
                )
            else:
                second[h, n] = push(
                    mid.at[1, :, far_z], relay.at[:, z], p2_send.at[1, n], p2_recv.at[1, n], on(y, far_z, c)
                )
        if h == 0:
            share_own(0, 0, mid.at[0, y])
            keep[2].start()
        else:
            share_other(0, 0, mid.at[1, :, z])
    for n, k in NEAREST:
        second[0, n].wait_recv()
        share_own(n + 1, k, None)
    for n, k in NEAREST:
        second[1, n].wait_recv()
        share_other(n + 1, k, None)
    pass_own(0, 0)
    for n, k in NEAREST:
        pass_own(n + 1, k)
    for n in (0,) + tuple(n + 1 for n, k in NEAREST):
        wait_for(b_recv.at[1, n])
        pass_other(n).start()
    keep[2].wait()
    for n in range(RING):
        wait_for(a_recv.at[1, n])
        wait_for(b_recv.at[0, n])
        wait_for(b_recv.at[2, n])

    def operands(pair, time, j):
        d = [
            jnp.concatenate([full[2 * time + b, :, jj, zz].reshape(16, 128) for jj in (j, j + 1) for zz in range(RING)], axis=0)
            for b in range(2)
        ]
        moved = jnp.dot(jnp.concatenate(d, axis=1), perm[...], preferred_element_type=F32).astype(BF16)
        for jj in range(2):
            for ch in range(2):
                for part in range(2):
                    rhs[pair, ch, part * 128:(part + 1) * 128, (j + jj) * 128:(j + jj + 1) * 128] = moved[
                        jj * 128:(jj + 1) * 128, part * 256 + ch * 128:part * 256 + (ch + 1) * 128
                    ]

    def fold(pair, zz):
        rows = pl.ds(pl.multiple_of(zz * 16, 16), 16)
        for ch in range(2):
            x = [rhs[pair, ch, rows, i * 128:(i + 1) * 128].astype(F32) for i in range(8)]
            for e in range(CELL_DEV):
                place = pl.ds(pl.multiple_of(e * 128 + zz * 16, 16), 16)
                for j in range(8):
                    acc = None
                    for i in range(j + 1):
                        t = i * 8 - i * (i - 1) // 2 + j - i
                        term = x[i] * wsm[ch, e, t]
                        acc = term if acc is None else acc + term
                    lhs[pair, ch, place, j * 128:(j + 1) * 128] = acc.astype(BF16)

    def products(pair, time):
        def slab(zz, carry):
            fold(pair, zz)
            return carry

        for j in range(0, 8, 2):
            operands(pair, time, j)
        lax.fori_loop(0, RING, slab, 0)
        for ch in range(2):
            result = lax.dot_general(
                lhs[pair, ch], rhs[pair, ch], (((1,), (1,)), ((), ())), preferred_element_type=F32
            )
            for e in range(CELL_DEV):
                for x in range(2):
                    value = result[e * 128:(e + 1) * 128, x * 128:(x + 1) * 128]
                    out[e, ch, x] = value if pair == 0 else out[e, ch, x] + value

    products(0, bl // 2)
    for n in range(RING):
        wait_for(a_recv.at[2, n])
        wait_for(b_recv.at[3, n])
    products(1, 1 - bl // 2)

    for copy in sent:
        copy.wait_send()
    for n in range(RING):
        pass_other(n).wait_send()


def shards(samples, history, tile_cell, tile_weight):
    table = jnp.asarray(filter_table())
    hbm = pl.BlockSpec(memory_space=pltpu.HBM)
    dma = pltpu.SemaphoreType.DMA
    return pl.pallas_call(
        kernel,
        out_shape=jax.ShapeDtypeStruct((CELL_DEV, 2, 2, BLOCK, BLOCK), F32),
        in_specs=[hbm] * 5,
        out_specs=pl.BlockSpec(memory_space=pltpu.VMEM),
        scratch_shapes=[
            pltpu.VMEM((2 * CH, TAPS * FRAME), BF16),
            pltpu.VMEM((8, SPEC_DEV * FRAME), BF16),
            pltpu.VMEM((8, HALO * FRAME), BF16),
            pltpu.VMEM((8 * SPEC_DEV, TAPS * FRAME), BF16),
            pltpu.VMEM((512, 256), F32),
            pltpu.VMEM((1024, 128), F32),
            pltpu.VMEM((2, RING, RING, 8, 128), BF16),
            pltpu.VMEM((2, RING, RING, 8, 128), BF16),
            pltpu.VMEM((RING, RING, 8, 128), BF16),
            pltpu.VMEM((NX, 2, RING, RING, 8, 128), BF16),
            pltpu.VMEM((256, 512), BF16),
            pltpu.VMEM((2, 2, 256, 1024), BF16),
            pltpu.VMEM((2, 2, 256, 1024), BF16),
            pltpu.SMEM((2, CELL_DEV, NTILE), F32),
            pltpu.SMEM((2, NTILE), jnp.int32),
            pltpu.SMEM((2, NTILE), F32),
            dma,
            dma,
            dma((2,)),
            dma,
            dma,
            dma((5,)),
            dma((2, RING - 1)),
            dma((2, RING - 1)),
            dma((2, RING - 1)),
            dma((2, RING - 1)),
            dma((3, RING)),
            dma((3, RING)),
            dma((4, RING)),
            dma((4, RING)),
        ],
        compiler_params=pltpu.CompilerParams(
            collective_id=0, has_side_effects=True, vmem_limit_bytes=40 * 1024 * 1024
        ),
    )(*[pltpu.with_memory_space_constraint(v, pltpu.HBM) for v in (samples, history, table, tile_cell, tile_weight)])


def solution(mesh):
    return jax.shard_map(
        shards,
        mesh=mesh,
        in_specs=(P("ct", "bl"), P("ct", None), P("ct", None), P("ct", None)),
        out_specs=P("bl", "ct", None, None, None),
        check_vma=False,
    )
```

```python
import functools
import math

import jax
import jax.numpy as jnp
import numpy as np
from jax import lax
from jax.experimental import pallas as pl
from jax.experimental.pallas import tpu as pltpu
from jax.sharding import PartitionSpec as P

MESH = pl.DeviceIdType.MESH
BF16 = jnp.bfloat16
F32 = jnp.float32

CH = 256
BLOCK = 128
TAPS = 4
SPECTRA = 128
FRAME = 512
NTILE = 36
CELL_DEV = 2
RING = 8
NX = 4
ROWS = 8
SPEC_DEV = SPECTRA // NX
HALO = TAPS - 1


def offset(n):
    m = n - 1
    odd = m % 2
    return (1 - (n == 0)) * (4 + (1 - odd) * (m // 2) - odd * ((m + 1) // 2))


OFFSETS = tuple(offset(n) for n in range(1, RING))
NEAREST = tuple(reversed(tuple(enumerate(OFFSETS))))


def filter_table():
    span = TAPS * FRAME
    pos = np.arange(span, dtype=np.float32) + np.float32(0.5)
    window = np.sinc(pos / np.float32(FRAME) - np.float32(TAPS / 2.0)).astype(np.float32) * (
        np.float32(0.5) - np.float32(0.5) * np.cos(np.float32(2.0 * math.pi) * pos / np.float32(span))
    )
    phase = np.arange(FRAME)[:, None] * np.arange(CH)[None, :] % FRAME
    angle = phase.astype(np.float32) * np.float32(2.0 * math.pi / FRAME)
    basis = np.concatenate([np.cos(angle), -np.sin(angle)], axis=1).astype(np.float32)
    table = window.astype(np.float32).reshape(TAPS, FRAME)[:, :, None] * basis[None]
    table = table * np.float32(2.0 / math.sqrt(FRAME))
    part, core, chip = np.meshgrid(np.arange(4), np.arange(2), np.arange(64), indexing="ij")
    column = (part % 2) * CH + 2 * (2 * chip + core) + part // 2
    rows = table[:, :, column.reshape(-1)].transpose(2, 0, 1).reshape(2 * CH, span)
    return np.ascontiguousarray(rows).astype(BF16)


def swap_step(pair, bit, lane):
    low, high = pair
    clear = (lane & bit) == 0
    return (
        jnp.where(clear, low, pltpu.roll(high, bit, 1)),
        jnp.where(clear, pltpu.roll(low, 128 - bit, 1), high),
    )


def kernel(
    samples, history, table, cells_hbm, weights_hbm, out,
    tab, smp, halo, taps, spec, turn, hold, mid, relay, full, perm, rhs, lhs, wsm, cells, weights,
    tab_sem, smp_sem, cell_sem, halo_send, halo_recv, own_sem, p1_send, p1_recv, p2_send, p2_recv, a_send, a_recv,
    b_send, b_recv,
):
    ct = lax.axis_index("ct")
    bl = lax.axis_index("bl")
    y = ct // 16
    z = lax.rem(ct // 2, RING)
    c = lax.rem(ct, 2)

    def on(yy, zz, cc):
        return (yy * 16 + zz * 2 + cc, bl)

    barrier = pltpu.get_barrier_semaphore()

    def greet(device):
        pl.semaphore_signal(barrier, inc=1, device_id=device, device_id_type=MESH)

    for k in (1, NX - 1):
        greet((ct, lax.rem(bl + k, NX)))
        greet(on(y, z, 1 - c)[:1] + (lax.rem(bl + k, NX),))
    greet(on(y, z, 1 - c))
    for k in range(1, RING):
        greet(on(lax.rem(y + k, RING), z, c))
        greet(on(y, lax.rem(z + k, RING), c))

    smp_copy = pltpu.make_async_copy(samples, smp, smp_sem)
    smp_copy.start()
    cell_copies = [
        pltpu.make_async_copy(cells_hbm, cells, cell_sem.at[0]),
        pltpu.make_async_copy(weights_hbm, weights, cell_sem.at[1]),
    ]
    for copy in cell_copies:
        copy.start()
    tab_copy = pltpu.make_async_copy(table, tab, tab_sem)
    tab_copy.start()

    pl.semaphore_wait(barrier, 5 + 2 * (RING - 1))

    halo_copy = pltpu.make_async_remote_copy(
        src_ref=samples.at[:, pl.ds((SPEC_DEV - HALO) * FRAME, HALO * FRAME)],
        dst_ref=halo,
        send_sem=halo_send,
        recv_sem=halo_recv,
        device_id=(ct, lax.rem(bl + 1, NX)),
        device_id_type=MESH,
    )
    hist_copy = pltpu.make_async_copy(history, halo, own_sem.at[4])

    @pl.when(bl < NX - 1)
    def _():
        halo_copy.start()

    @pl.when(bl == 0)
    def _():
        hist_copy.start()

    def put(ext, value):
        for t in range(TAPS):
            if 0 <= ext - t < SPEC_DEV:
                taps[pl.ds(8 * (ext - t), 8), t * FRAME:(t + 1) * FRAME] = value

    smp_copy.wait()
    for f in range(SPEC_DEV):
        put(f + HALO, smp[:, pl.ds(f * FRAME, FRAME)])

    @pl.when(bl < NX - 1)
    def _():
        halo_copy.wait_send()

    @pl.when(bl == 0)
    def _():
        hist_copy.wait()

    @pl.when(bl > 0)
    def _():
        halo_copy.wait_recv()

    for f in range(HALO):
        put(f, halo[:, pl.ds(f * FRAME, FRAME)])

    tab_copy.wait()
    spec[...] = lax.dot_general(tab[...], taps[...], (((1,), (1,)), ((), ())), preferred_element_type=F32)

    lane = lax.broadcasted_iota(jnp.int32, (8, 128), 1)
    def column(k):
        return lax.rem(y + RING - k, RING)

    def depth(k):
        return lax.rem(z + RING - k, RING)

    def to_rows(core, which, chips):
        at = core * 64 + chips * 8
        v = [
            spec[pl.ds(pl.multiple_of(q * 128 + at, 8), 8), pl.ds(h * 128, 128)]
            for q in range(4)
            for h in range(2)
        ]
        for bit in (1, 2, 4):
            for i in range(8):
                if not i & bit:
                    v[i], v[i | bit] = swap_step((v[i], v[i | bit]), bit, lane)
        place = which * 512 + chips * 64
        for p in range(ROWS):
            turn[pl.ds(place + p, 8, stride=8), :] = v[p]
        hold[which, chips] = turn[pl.ds(place, 64), :].astype(BF16).reshape(8, 8, 128)

    first = {}
    for chips in range(8):
        to_rows(c, 0, chips)
    for n, k in enumerate(OFFSETS):
        far_z = lax.rem(z + k, RING)
        first[0, n] = pltpu.make_async_remote_copy(
            src_ref=hold.at[0, :, far_z], dst_ref=mid.at[0, :, z],
            send_sem=p1_send.at[0, n], recv_sem=p1_recv.at[0, n], device_id=on(y, far_z, c), device_id_type=MESH,
        )
        first[0, n].start()
    for chips in range(8):
        to_rows(1 - c, 1, chips)
    for n, k in enumerate(OFFSETS):
        far_y = lax.rem(y + k, RING)
        first[1, n] = pltpu.make_async_remote_copy(
            src_ref=hold.at[1, far_y], dst_ref=mid.at[1, y],
            send_sem=p1_send.at[1, n], recv_sem=p1_recv.at[1, n], device_id=on(far_y, z, c), device_id_type=MESH,
        )
        first[1, n].start()
    keep = [
        pltpu.make_async_copy(hold.at[0, :, z], mid.at[0, :, z], own_sem.at[0]),
        pltpu.make_async_copy(hold.at[1, y], mid.at[1, y], own_sem.at[1]),
        pltpu.make_async_copy(mid.at[0, y], full.at[bl, c, y], own_sem.at[2]),
    ]
    keep[0].start()
    keep[1].start()

    for copy in cell_copies:
        copy.wait()

    def one_weight(t, carry):
        for ch in range(2):
            scaled = weights[ch, t] * (1.0 / math.sqrt(SPECTRA))
            for e in range(CELL_DEV):
                wsm[ch, e, t] = jnp.where(cells[ch, t] == bl * CELL_DEV + e, scaled, 0.0)
        return carry

    lax.fori_loop(0, NTILE, one_weight, 0)

    source = lax.broadcasted_iota(jnp.int32, (256, 512), 0)
    column_id = lax.broadcasted_iota(jnp.int32, (256, 512), 1)
    turned, channel = column_id // 256, (column_id // 128) % 2
    lane_id = (column_id % 128) ^ (2 * turned)
    wanted = ((lane_id // 4) % 2) * 128 + (lane_id & 123) + 4 * channel
    sign = 1 - 2 * turned * (lane_id // 2 % 2)
    perm[...] = jnp.where(source == wanted, sign, 0).astype(F32).astype(BF16)

    right, left = lax.rem(bl + 1, NX), lax.rem(bl + NX - 1, NX)
    sent = list(first.values())

    def push(source, target, send, recv, device):
        copy = pltpu.make_async_remote_copy(
            src_ref=source, dst_ref=target, send_sem=send, recv_sem=recv, device_id=device, device_id_type=MESH
        )
        copy.start()
        sent.append(copy)
        return copy

    def wait_for(sem):
        pltpu.make_async_remote_copy(
            src_ref=relay.at[0], dst_ref=relay.at[0], send_sem=own_sem.at[3], recv_sem=sem,
            device_id=(ct, right), device_id_type=MESH,
        ).wait_recv()

    def share_own(n, k, source):
        target = full.at[bl, c, column(k)]
        source = target if source is None else source
        push(source, target, a_send.at[0, n], a_recv.at[0, n], (ct, right))
        push(source, target, a_send.at[1, n], a_recv.at[1, n], (ct, left))

    def share_other(n, k, source):
        target = full.at[bl, c, :, depth(k)]
        source = relay.at[:, depth(k)] if source is None else source
        push(source, target, b_send.at[0, n], b_recv.at[0, n], on(y, z, 1 - c)[:1] + (right,))
        push(source, target, b_send.at[1, n], b_recv.at[1, n], on(y, z, 1 - c)[:1] + (left,))
        push(source, target, b_send.at[2, n], b_recv.at[2, n], on(y, z, 1 - c))

    def pass_own(n, k):
        wait_for(a_recv.at[0, n])
        chunk = full.at[left, c, column(k)]
        push(chunk, chunk, a_send.at[2, n], a_recv.at[2, n], (ct, right))

    def pass_other(n):
        chunk = full.at[right, 1 - c, :, depth(offset(n))]
        return pltpu.make_async_remote_copy(
            src_ref=chunk, dst_ref=chunk, send_sem=b_send.at[3, n], recv_sem=b_recv.at[3, n],
            device_id=(ct, left), device_id_type=MESH,
        )

    second = {}
    for h in range(2):
        for n in range(RING - 1):
            first[h, n].wait_recv()
        keep[h].wait()
        for n, k in enumerate(OFFSETS):
            far_y, far_z = lax.rem(y + k, RING), lax.rem(z + k, RING)
            if h == 0:
                second[h, n] = push(
                    mid.at[0, far_y], full.at[bl, c, y], p2_send.at[0, n], p2_recv.at[0, n], on(far_y, z, c)
                )
            else:
                second[h, n] = push(
                    mid.at[1, :, far_z], relay.at[:, z], p2_send.at[1, n], p2_recv.at[1, n], on(y, far_z, c)
                )
        if h == 0:
            share_own(0, 0, mid.at[0, y])
            keep[2].start()
        else:
            share_other(0, 0, mid.at[1, :, z])
    for n, k in NEAREST:
        second[0, n].wait_recv()
        share_own(n + 1, k, None)
    for n, k in NEAREST:
        second[1, n].wait_recv()
        share_other(n + 1, k, None)
    order = ((-1, 0),) + NEAREST
    for i in range(RING + 3):
        if i < RING:
            pass_own(order[i][0] + 1, order[i][1])
        if i >= 3:
            n = order[i - 3][0] + 1
            wait_for(b_recv.at[1, n])
            pass_other(n).start()
    keep[2].wait()
    for n in range(RING):
        wait_for(a_recv.at[1, n])
        wait_for(b_recv.at[0, n])
        wait_for(b_recv.at[2, n])

    def operands(pair, time, j):
        d = [
            jnp.concatenate([full[2 * time + b, :, jj, zz].reshape(16, 128) for jj in (j, j + 1) for zz in range(RING)], axis=0)
            for b in range(2)
        ]
        moved = jnp.dot(jnp.concatenate(d, axis=1), perm[...], preferred_element_type=F32).astype(BF16)
        for jj in range(2):
            for ch in range(2):
                for part in range(2):
                    rhs[pair, ch, part * 128:(part + 1) * 128, (j + jj) * 128:(j + jj + 1) * 128] = moved[
                        jj * 128:(jj + 1) * 128, part * 256 + ch * 128:part * 256 + (ch + 1) * 128
                    ]

    def fold(pair, zz):
        rows = pl.ds(pl.multiple_of(zz * 16, 16), 16)
        for ch in range(2):
            x = [rhs[pair, ch, rows, i * 128:(i + 1) * 128].astype(F32) for i in range(8)]
            for e in range(CELL_DEV):
                place = pl.ds(pl.multiple_of(e * 128 + zz * 16, 16), 16)
                for j in range(8):
                    acc = None
                    for i in range(j + 1):
                        t = i * 8 - i * (i - 1) // 2 + j - i
                        term = x[i] * wsm[ch, e, t]
                        acc = term if acc is None else acc + term
                    lhs[pair, ch, place, j * 128:(j + 1) * 128] = acc.astype(BF16)

    def products(pair, time):
        def slab(zz, carry):
            fold(pair, zz)
            return carry

        for j in range(0, 8, 2):
            operands(pair, time, j)
        lax.fori_loop(0, RING, slab, 0)
        for ch in range(2):
            result = lax.dot_general(
                lhs[pair, ch], rhs[pair, ch], (((1,), (1,)), ((), ())), preferred_element_type=F32
            )
            for e in range(CELL_DEV):
                for x in range(2):
                    value = result[e * 128:(e + 1) * 128, x * 128:(x + 1) * 128]
                    out[e, ch, x] = value if pair == 0 else out[e, ch, x] + value

    products(0, bl // 2)
    for n in range(RING):
        wait_for(a_recv.at[2, n])
        wait_for(b_recv.at[3, n])
    products(1, 1 - bl // 2)

    for copy in sent:
        copy.wait_send()
    for n in range(RING):
        pass_other(n).wait_send()


def shards(samples, history, tile_cell, tile_weight):
    table = jnp.asarray(filter_table())
    hbm = pl.BlockSpec(memory_space=pltpu.HBM)
    dma = pltpu.SemaphoreType.DMA
    return pl.pallas_call(
        kernel,
        out_shape=jax.ShapeDtypeStruct((CELL_DEV, 2, 2, BLOCK, BLOCK), F32),
        in_specs=[hbm] * 5,
        out_specs=pl.BlockSpec(memory_space=pltpu.VMEM),
        scratch_shapes=[
            pltpu.VMEM((2 * CH, TAPS * FRAME), BF16),
            pltpu.VMEM((8, SPEC_DEV * FRAME), BF16),
            pltpu.VMEM((8, HALO * FRAME), BF16),
            pltpu.VMEM((8 * SPEC_DEV, TAPS * FRAME), BF16),
            pltpu.VMEM((512, 256), F32),
            pltpu.VMEM((1024, 128), F32),
            pltpu.VMEM((2, RING, RING, 8, 128), BF16),
            pltpu.VMEM((2, RING, RING, 8, 128), BF16),
            pltpu.VMEM((RING, RING, 8, 128), BF16),
            pltpu.VMEM((NX, 2, RING, RING, 8, 128), BF16),
            pltpu.VMEM((256, 512), BF16),
            pltpu.VMEM((2, 2, 256, 1024), BF16),
            pltpu.VMEM((2, 2, 256, 1024), BF16),
            pltpu.SMEM((2, CELL_DEV, NTILE), F32),
            pltpu.SMEM((2, NTILE), jnp.int32),
            pltpu.SMEM((2, NTILE), F32),
            dma,
            dma,
            dma((2,)),
            dma,
            dma,
            dma((5,)),
            dma((2, RING - 1)),
            dma((2, RING - 1)),
            dma((2, RING - 1)),
            dma((2, RING - 1)),
            dma((3, RING)),
            dma((3, RING)),
            dma((4, RING)),
            dma((4, RING)),
        ],
        compiler_params=pltpu.CompilerParams(
            collective_id=0, has_side_effects=True, vmem_limit_bytes=40 * 1024 * 1024
        ),
    )(*[pltpu.with_memory_space_constraint(v, pltpu.HBM) for v in (samples, history, table, tile_cell, tile_weight)])


def solution(mesh):
    return jax.shard_map(
        shards,
        mesh=mesh,
        in_specs=(P("ct", "bl"), P("ct", None), P("ct", None), P("ct", None)),
        out_specs=P("bl", "ct", None, None, None),
        check_vma=False,
    )
```
